768 devices in a mesh: grp: 16 (over y, core), sub: 48 (over z, x).
Axes of the slice: x: 4, y: 8, z: 12, core: 2. Of those that a mesh axis runs over, the one named last changes fastest.
Arguments:
- charges: float32 [16, 3145728], P(None, ('grp', 'sub')), may hold values from -6 to 6
- centers: float32 [3, 3145728], P(None, ('grp', 'sub')), may hold values from 0 to 770
- areas: float32 [3145728], P(('grp', 'sub')), may hold values from 0.1 to 0.4
- panel_count: int32 [12288], P(('grp', 'sub')), may hold values from 192 to 256
- near_pairs: int32 [2, 24576], P(None, ('grp', 'sub')), may hold values from 0 to 31, as said below
- pair_count: int32 [768], P(('grp', 'sub')), may hold values from 8 to 32, as said below
- basis: float32 [12288, 32, 256], P(('grp', 'sub')), may hold values from -0.375 to 0.375
- leaf_transfer: float32 [12288, 32, 32], P(('grp', 'sub')), may hold values from -0.25 to 0.25
- cluster_transfer: float32 [768, 32, 32], P(('grp', 'sub')), may hold values from -0.15625 to 0.15625
- leaf_coupling: float32 [12288, 32, 1024], P(('grp', 'sub')), may hold values from -0.1875 to 0.1875
- cluster_coupling: float32 [768, 32, 1536], P(('grp', 'sub')), may hold values from -0.4375 to 0.4375
- group_coupling: float32 [16, 32, 512], replicated, may hold values from -6 to 6
Outputs:
- potential: float32 [16, 3145728], P(None, ('grp', 'sub'))
The draws below stay inside these ranges and needn't reach their ends.
Inputs may be any that keep to these rules, and one draw needn't show every extreme that they name: `near_pairs`: each device has 32 distinct slots (u, w) with u < 16 and u < w; positions w of 16 or more name leaves of the next device along sub and never occur on the last device of a grp group. Device d uses its first pair_count[d] slots; some device uses all 32.
All inputs are finite; a program needn't handle non-finite values.
Results may differ from the reference program's by a relative error of at most 0.0003.
Values sent between devices are 32-bit elements; how exact they have to be, the bound alone decides.
No kernel may reach another device: no remote copies, remote signals or barrier semaphores. Data moves between devices by JAX's collectives and lax.ppermute only.
A program may use at most 64 MiB of HBM per device.

```python
import math
import jax
import jax.numpy as jnp
import numpy as np
from jax import lax

LEAF = 256
RANK = 32
RHS = 16
LEAVES_DEV = 16
PAIRS_DEV = 32
LEAVES = 12288
PANELS = 3145728
N_GRP = 16
N_SUB = 48
DEVICES = 768


def pair_table():
    inner_pairs = [(a, w) for a in range(LEAVES_DEV) for w in range(a + 1, LEAVES_DEV)]
    cross_pairs = [(a, LEAVES_DEV + b) for a in range(LEAVES_DEV) for b in range(LEAVES_DEV)]
    return (np.array(inner_pairs + cross_pairs, dtype=np.int32), len(inner_pairs))


def draw_near_pairs(key, part):
    key = jax.random.fold_in(key, 5)
    candidates, inner_count = pair_table()
    candidate_count = candidates.shape[0]
    device_total = N_GRP * N_SUB
    device_keys = jax.random.split(key, device_total)

    def shuffled(single_key):
        return jax.random.permutation(single_key, candidate_count)
    rank_order = jax.vmap(shuffled)(device_keys).astype(jnp.int32)
    last_device = (jnp.arange(device_total, dtype=jnp.int32) % N_SUB == N_SUB - 1).astype(jnp.int32)
    crossing = (jnp.arange(candidate_count, dtype=jnp.int32) >= inner_count).astype(jnp.int32)
    ordering = rank_order + candidate_count * last_device[:, None] * crossing[None, :]
    sorted_index = jnp.argsort(ordering, axis=1, stable=True)[:, :PAIRS_DEV]
    chosen = jnp.asarray(candidates)[sorted_index]
    return jnp.transpose(chosen, (2, 0, 1)).reshape(2, device_total * PAIRS_DEV).astype(jnp.int32)


def draw_pair_count(key, part):
    key = jax.random.fold_in(key, 7)
    count_key, pick_key = jax.random.split(key)
    device_total = N_GRP * N_SUB
    slot_counts = jax.random.randint(count_key, (device_total,), PAIRS_DEV // 4, PAIRS_DEV + 1)
    chosen = jax.random.randint(pick_key, (), 0, device_total)
    return jnp.where(jnp.arange(device_total) == chosen, PAIRS_DEV, slot_counts).astype(jnp.int32)


def draw_centers(key, part):
    key = jax.random.fold_in(key, 3)
    leaf_index = jnp.arange(PANELS, dtype=jnp.int32) // LEAF
    lattice = jnp.stack([leaf_index % 4, leaf_index // 4 % 4, leaf_index // 16]).astype(jnp.float32) * 0.7
    jitter = jax.random.uniform(key, (3, PANELS), jnp.float32)
    return lattice + jitter


def touch_ends(values, key, least, top_value):
    shape = values.shape
    index_at = [jax.random.randint(jax.random.fold_in(key, axis), (), 0, shape[axis]) for axis in range(len(shape))]
    values = values.at[tuple(index_at)].set(least)
    longest = shape.index(max(shape))
    index_at[longest] = (index_at[longest] + 1) % shape[longest]
    return values.at[tuple(index_at)].set(top_value)


def shard_levels(key, extent, shards, smallest, high):
    loudness, own = 1.0, jax.random.fold_in(key, 6)
    for position, blocks in shards:
        heights = jnp.exp(jax.random.uniform(jax.random.fold_in(own, position), (blocks,), jnp.float32, smallest / len(shards), high / len(shards)))
        loudness = loudness * jnp.repeat(heights, extent[position] // blocks).reshape([-1 if axis == position else 1 for axis in range(len(extent))])
    return loudness


def normal_values(key, extent, scale, bound, cuts=(), kind=jnp.bfloat16):
    gain = shard_levels(key, extent, cuts, -0.22, 0.18) if cuts else 1.0
    values = jax.random.normal(key, extent, jnp.float32) * scale * gain
    return jnp.minimum(jnp.maximum(values, -bound), bound).astype(kind)


def setup_inputs(seed: int = 0) -> dict:
    key_of = jax.random.split(jax.random.key(seed), 13)
    return {
        "charges": normal_values(key_of[0], (RHS, PANELS), 1.0, 6.0, ((1, 768),), jnp.float32),
        "centers": draw_centers(jax.random.fold_in(key_of[12], 71), 0),
        "areas": jnp.clip(jnp.exp(math.log(0.4) - 1.3862944 * jax.random.uniform(key_of[2], (PANELS,), jnp.float32) ** shard_levels(key_of[2], (PANELS,), ((0, 768),), -0.2, 0.2)), 0.1, 0.4),
        "panel_count": touch_ends(jax.random.randint(key_of[3], (LEAVES,), LEAF * 3 // 4, LEAF + 1), jax.random.fold_in(key_of[3], 1), LEAF * 3 // 4, LEAF).astype(jnp.int32),
        "near_pairs": draw_near_pairs(jax.random.fold_in(key_of[12], 71), 0),
        "pair_count": draw_pair_count(jax.random.fold_in(key_of[12], 71), 0),
        "basis": normal_values(key_of[6], (LEAVES, RANK, LEAF), LEAF ** -0.5, 0.375, ((0, 768),), jnp.float32),
        "leaf_transfer": normal_values(key_of[7], (LEAVES, RANK, RANK), (RANK * LEAVES_DEV) ** -0.5, 0.25, ((0, 768),), jnp.float32),
        "cluster_transfer": normal_values(key_of[8], (DEVICES, RANK, RANK), (RANK * N_SUB) ** -0.5, 0.15625, ((0, 768),), jnp.float32),
        "leaf_coupling": normal_values(key_of[9], (LEAVES, RANK, 2 * LEAVES_DEV * RANK), (RANK * LEAVES_DEV * 2) ** -0.5, 0.1875, ((0, 768),), jnp.float32),
        "cluster_coupling": normal_values(key_of[10], (DEVICES, RANK, N_SUB * RANK), (RANK * N_SUB // 9 + 1) ** -0.5, 0.4375, ((0, 768),), jnp.float32),
        "group_coupling": normal_values(key_of[11], (N_GRP, RANK, N_GRP * RANK), 1.0, 6.0, (), jnp.float32),
    }


SOFTENING = 0.05
precise = lax.Precision.HIGHEST

def kernel_blocks(source_place, source_weight, target_place, target_weight):
    squared = (source_place[0][:, :, None] - target_place[0][:, None, :]) ** 2
    squared = squared + (source_place[1][:, :, None] - target_place[1][:, None, :]) ** 2
    squared = squared + (source_place[2][:, :, None] - target_place[2][:, None, :]) ** 2
    return source_weight[:, :, None] * target_weight[:, None, :] * lax.rsqrt(squared + SOFTENING)

def one_hot(index, count):
    return (index[:, None] == jnp.arange(count, dtype=jnp.int32)[None, :]).astype(jnp.float32)

def upper_mask(count, offset):
    steps = jnp.arange(count, dtype=jnp.int32)
    return (steps[None, :] >= steps[:, None] + offset).astype(jnp.float32)

def reference(charges, centers, areas, panel_count, near_pairs, pair_count, basis, leaf_transfer, cluster_transfer, leaf_coupling, cluster_coupling, group_coupling):
    devices = N_GRP * N_SUB
    leaves = LEAVES_DEV * devices
    slots = PAIRS_DEV
    width = 2 * LEAVES_DEV
    inside = (jnp.arange(LEAF, dtype=jnp.int32)[None, :] < panel_count[:, None]).astype(jnp.float32)
    masked_weight = areas.reshape(leaves, LEAF) * inside
    masked_charge = charges.reshape(RHS, leaves, LEAF) * inside[None]
    places = centers.reshape(3, leaves, LEAF)
    coefficients = jnp.einsum('arp,nap->arn', basis, masked_charge, precision=precise)
    cluster = jnp.einsum('ars,arn->asn', leaf_transfer, coefficients, precision=precise)
    cluster = cluster.reshape(devices, LEAVES_DEV, RANK, RHS).sum(1)
    lifted = jnp.einsum('drs,drn->dsn', cluster_transfer, cluster, precision=precise)
    lifted = lifted.reshape(N_GRP, N_SUB, RANK, RHS).sum(1)
    group_matrix = group_coupling.reshape(N_GRP, RANK, N_GRP, RANK) * upper_mask(N_GRP, 1)[:, None, :, None]
    group_field = jnp.einsum('arbs,bsn->arn', group_matrix, lifted, precision=precise)
    group_field = group_field + jnp.einsum('bsar,bsn->arn', group_matrix, lifted, precision=precise)
    sub_matrix = cluster_coupling.reshape(N_GRP, N_SUB, RANK, N_SUB, RANK) * upper_mask(N_SUB, 2)[None, :, None, :, None]
    grouped = cluster.reshape(N_GRP, N_SUB, RANK, RHS)
    cluster_field = jnp.einsum('gasbt,gbtn->gasn', sub_matrix, grouped, precision=precise)
    cluster_field = cluster_field + jnp.einsum('gbtas,gbtn->gasn', sub_matrix, grouped, precision=precise)
    cluster_field = cluster_field.reshape(devices, RANK, RHS)
    cluster_field = cluster_field + jnp.einsum('drs,dsn->drn', cluster_transfer, jnp.repeat(group_field, N_SUB, axis=0), precision=precise)
    window_upper = (jnp.arange(width, dtype=jnp.int32)[None, :] > jnp.arange(LEAVES_DEV, dtype=jnp.int32)[:, None]).astype(jnp.float32)

    def device_part(device):
        first_leaf = device * LEAVES_DEV
        window = jnp.minimum(first_leaf + jnp.arange(width, dtype=jnp.int32), leaves - 1)
        exists = ((jnp.arange(width, dtype=jnp.int32) < LEAVES_DEV) | (device % N_SUB != N_SUB - 1)).astype(jnp.float32)
        window_place = places[:, window]
        window_weight = masked_weight[window] * exists[:, None]
        window_charge = masked_charge[:, window] * exists[None, :, None]
        window_coefs = coefficients[window] * exists[:, None, None]
        pair_source = lax.dynamic_slice_in_dim(near_pairs[0], device * slots, slots)
        pair_target = lax.dynamic_slice_in_dim(near_pairs[1], device * slots, slots)
        live_slot = (jnp.arange(slots, dtype=jnp.int32) < pair_count[device]).astype(jnp.float32)
        own_leaf = jnp.arange(LEAVES_DEV, dtype=jnp.int32)
        source = jnp.concatenate([pair_source, own_leaf])
        target = jnp.concatenate([pair_target, own_leaf])
        usage_mask = jnp.concatenate([live_slot, jnp.ones((LEAVES_DEV,), jnp.float32)])
        mirror = jnp.concatenate([live_slot, jnp.zeros((LEAVES_DEV,), jnp.float32)])
        blocks = kernel_blocks(window_place[:, source], window_weight[source], window_place[:, target], window_weight[target])
        forward = jnp.einsum('spq,nsq->snp', blocks, window_charge[:, target], precision=precise) * usage_mask[:, None, None]
        backward = jnp.einsum('spq,nsp->snq', blocks, window_charge[:, source], precision=precise) * mirror[:, None, None]
        near_field = jnp.einsum('sw,snp->nwp', one_hot(source, width), forward, precision=precise)
        near_field = near_field + jnp.einsum('sw,snp->nwp', one_hot(target, width), backward, precision=precise)
        listed = jnp.einsum('s,sa,sw->aw', live_slot, one_hot(pair_source, LEAVES_DEV), one_hot(pair_target, width), precision=precise)
        far_mask = window_upper * (1.0 - listed) * exists[None, :]
        coupling = lax.dynamic_slice_in_dim(leaf_coupling, first_leaf, LEAVES_DEV).reshape(LEAVES_DEV, RANK, width, RANK)
        own_coefs = lax.dynamic_slice_in_dim(coefficients, first_leaf, LEAVES_DEV)
        incoming = jnp.einsum('arwk,aw,wkn->arn', coupling, far_mask, window_coefs, precision=precise)
        outgoing = jnp.einsum('arwk,aw,arn->wkn', coupling, far_mask, own_coefs, precision=precise)
        return (near_field[:, :LEAVES_DEV], near_field[:, LEAVES_DEV:], incoming + outgoing[:LEAVES_DEV], outgoing[LEAVES_DEV:])
    near_own, near_next, leaf_field, far_next = lax.map(device_part, jnp.arange(devices, dtype=jnp.int32))
    opener = 1.0 - (jnp.arange(devices, dtype=jnp.int32) % N_SUB == 0).astype(jnp.float32)
    near_prev = jnp.concatenate([jnp.zeros_like(near_next[:1]), near_next[:-1]]) * opener[:, None, None, None]
    far_prev = jnp.concatenate([jnp.zeros_like(far_next[:1]), far_next[:-1]]) * opener[:, None, None, None]
    leaf_field = (leaf_field + far_prev).reshape(leaves, RANK, RHS)
    leaf_field = leaf_field + jnp.einsum('ars,asn->arn', leaf_transfer, jnp.repeat(cluster_field, LEAVES_DEV, axis=0), precision=precise)
    far_potential = jnp.einsum('arp,arn->nap', basis, leaf_field, precision=precise)
    near_total = jnp.transpose(near_own + near_prev, (1, 0, 2, 3)).reshape(RHS, leaves, LEAF)
    potential = (near_total + far_potential) * inside[None]
    return potential.reshape(RHS, leaves * LEAF)
```

```python
import functools

import jax
import jax.numpy as jnp
from jax import lax
from jax.experimental import pallas as pl
from jax.experimental.pallas import tpu as pltpu
from jax.sharding import PartitionSpec as P

SOFTENING = 0.05
LANES = 128
precise = lax.Precision.HIGHEST
f32 = jnp.float32
bf16 = jnp.bfloat16
NN = (((1,), (0,)), ((), ()))
NT = (((1,), (1,)), ((), ()))
TN = (((0,), (0,)), ((), ()))


def mm(a, b, dims=NN):
    return lax.dot_general(a, b, dims, precision=precise, preferred_element_type=f32)


def mm16(a, b, dims=NN):
    return lax.dot_general(a, b, dims, preferred_element_type=f32)


def lanes_of(shape):
    return lax.broadcasted_iota(jnp.int32, shape, len(shape) - 1)


def rolled(tile, shift):
    shift = shift % LANES
    return tile if shift == 0 else pltpu.roll(tile, shift, 1)


def inside_of(count_ref, leaf, panels):
    return lanes_of((1, panels)) < count_ref[leaf]


def upward(index, count, charges, areas, centers, basis, lt, ct, cc, z, x):
    sides, total = charges.shape
    leaves, rank, panels = basis.shape
    subs = z.shape[0]
    coefs = []
    for l in range(leaves):
        at = slice(l * panels, (l + 1) * panels)
        q = jnp.where(inside_of(count, l, panels), charges[:, at], 0.0)
        x[0:sides, at] = q * areas[:, at]
        coefs.append(mm(q, basis[l], NT))
    coefs = jnp.concatenate(coefs, axis=1)
    x[0:sides, total:] = coefs
    x[sides:, :] = jnp.zeros((x.shape[0] - sides, x.shape[1]), f32)
    x[sides : sides + 3, 0:total] = centers[...]
    cluster = mm(coefs, lt[...])
    lifted = mm(cluster, ct[...])
    product = mm(cluster, cc[...])
    half = sides // 2
    base = jnp.concatenate([cluster[:half], lifted[:half], cluster[half:], lifted[half:]], axis=1)
    lane = lanes_of((half, LANES))
    own = index[1]
    for e in range(subs):
        group, place = divmod(e * rank, LANES)
        at = slice(group * LANES, (group + 1) * LANES)
        low = rolled(product[:half, at], -place)
        high = rolled(product[half:, at], 2 * rank - place)
        piece = jnp.where(lane < rank, low, base)
        piece = jnp.where((lane >= 2 * rank) & (lane < 3 * rank), high, piece)
        z[e] = jnp.where(e > own, piece, base)


def inverse_distance(col, row):
    squared = (col[:, 0:1] - row[0:1, :]) ** 2 + SOFTENING
    squared = squared + (col[:, 1:2] - row[1:2, :]) ** 2
    squared = squared + (col[:, 2:3] - row[2:3, :]) ** 2
    return lax.rsqrt(squared)


def split(value):
    high = value.astype(bf16)
    return high, (value - high.astype(f32)).astype(bf16)


def stacked(value):
    high = value.astype(bf16).astype(f32)
    return jnp.concatenate([high, value - high], axis=0).astype(bf16)


def applied(charge, high, low, dims):
    both = mm16(charge, high, dims) + mm16(charge, low, dims)
    sides = both.shape[0] // 2
    return both[:sides] + both[sides:]


def own_blocks(index, x, basis, lt, ct, group, near, lifted_basis, group_matrix):
    sides, total = near.shape
    leaves, rank, panels = basis.shape
    groups = group.shape[0]
    g = index[0]

    @pl.loop(0, leaves)
    def _(i):
        at = pl.ds(pl.multiple_of(i * panels, panels), panels)
        places = x[sides : sides + 8, at]
        high, low = split(inverse_distance(places.T, places))
        near[:, at] = applied(stacked(x[0:sides, at]), high, low, NN)

    for l in range(leaves):
        lifted_basis[:, l * panels : (l + 1) * panels] = mm(
            lt[l * rank : (l + 1) * rank, :], basis[l], TN
        )
    transfer = ct[...]
    row = group[g]
    column_at = pl.ds(pl.multiple_of((g * rank) // LANES * LANES, LANES), LANES)
    place = (g * rank) % LANES
    for h in range(groups):
        block = row[:, h * rank : (h + 1) * rank]
        wide = group[h, :, column_at]
        column = wide[:, 0:rank]
        for k in range(1, LANES // rank):
            column = jnp.where(place == k * rank, wide[:, k * rank : (k + 1) * rank], column)
        later = mm(block, transfer, (((0,), (1,)), ((), ())))
        earlier = mm(column, transfer, NT)
        group_matrix[h * rank : (h + 1) * rank, :] = jnp.where(
            h > g, later, jnp.where(h < g, earlier, 0.0)
        )


def window_blocks(
    index, pairs, pair_count, x, x_next, coupling, near, out_next, far, charge, place, column, acc, masked
):
    sides, total = near.shape
    width, _, panels = acc.shape
    leaves = width // 2
    rank = far.shape[1] // leaves
    live = pair_count[0]

    for w in range(width):
        source = x if w < leaves else x_next
        at = slice(w % leaves * panels, (w % leaves + 1) * panels)
        charge[w] = stacked(source[0:sides, at])
        tile = source[sides : sides + 8, at]
        place[w] = tile
        if w < leaves:
            column[w] = tile.T
    acc[...] = jnp.zeros_like(acc)

    @pl.loop(0, live)
    def _(s):
        i, j = pairs[0, s], pairs[1, s]
        high, low = split(inverse_distance(column[i], place[j]))
        acc[i] += applied(charge[j], high, low, NT)
        acc[j] += applied(charge[i], high, low, NN)

    for l in range(leaves):
        at = slice(l * panels, (l + 1) * panels)
        near[:, at] = acc[l]
        out_next[:, at] = acc[leaves + l]

    lane_leaf = lanes_of((leaves, width * rank)) // rank
    row_leaf = lax.broadcasted_iota(jnp.int32, (leaves, width * rank), 0)
    has_next = index[2] > 0
    mask = jnp.where((lane_leaf > row_leaf) & ((lane_leaf < leaves) | has_next), 1.0, 0.0)

    def unlist(s, mask):
        return jnp.where((row_leaf == pairs[0, s]) & (lane_leaf == pairs[1, s]), 0.0, mask)

    mask = lax.fori_loop(0, live, unlist, mask)
    for l in range(leaves):
        at = slice(l * rank, (l + 1) * rank)
        masked[at, :] = coupling[at, :] * mask[l : l + 1, :]
    own = x[0:sides, total:]
    both = jnp.concatenate([own, x_next[0:sides, total:]], axis=1)
    outgoing = mm(own, masked[...])
    incoming = mm(both, masked[...], NT)
    far[...] = incoming + outgoing[:, : leaves * rank]
    out_next[:, total:] = outgoing[:, leaves * rank :]


def summed(got, out):
    total = jnp.sum(got[...], axis=0)
    for h in range(out.shape[0]):
        out[h] = total


def combined(
    index, count, got, cc, near_own, near_pairs, far, got_next, areas, basis, cluster, partial
):
    subs, half, _ = got.shape
    rank = cc.shape[0]
    sides = 2 * half
    leaves, _, panels = basis.shape
    total = areas.shape[1]
    own = index[1]
    behind = jnp.zeros((half, LANES), f32)
    lane = lanes_of((half, LANES))
    lows, highs = [], []
    per = LANES // rank
    for e in range(0, subs, per):
        low = high = jnp.zeros((half, LANES), f32)
        for k in range(per):
            tile = got[e + k]
            behind = behind + jnp.where(e + k + 2 <= own, tile, 0.0)
            tile = jnp.where(e + k >= own + 2, tile, 0.0)
            here = (lane >= k * rank) & (lane < (k + 1) * rank)
            low = jnp.where(here, rolled(tile, k * rank), low)
            high = jnp.where(here, rolled(tile, k * rank - 2 * rank), high)
        lows.append(low)
        highs.append(high)
    ahead = jnp.concatenate(
        [jnp.concatenate(lows, axis=1), jnp.concatenate(highs, axis=1)], axis=0
    )
    behind = jnp.concatenate([behind[:, :rank], behind[:, 2 * rank : 3 * rank]], axis=0)
    cluster[...] = behind + mm(ahead, cc[...], NT)
    field = far[...] + got_next[:, total:]
    for l in range(leaves):
        at = slice(l * panels, (l + 1) * panels)
        near = (near_own[:, at] + near_pairs[:, at] + got_next[:, at]) * areas[:, at]
        value = near + mm(field[:, l * rank : (l + 1) * rank], basis[l])
        partial[:, at] = jnp.where(inside_of(count, l, panels), value, 0.0)


def finished(count, got, cluster, group_matrix, lifted_basis, partial, potential):
    groups, half, _ = got.shape
    rank = lifted_basis.shape[0]
    leaves = count.shape[0]
    panels = partial.shape[1] // leaves
    low = jnp.concatenate([got[h][:, rank : 2 * rank] for h in range(groups)], axis=1)
    high = jnp.concatenate([got[h][:, 3 * rank : 4 * rank] for h in range(groups)], axis=1)
    field = cluster[...] + mm(jnp.concatenate([low, high], axis=0), group_matrix[...])
    value = mm(field, lifted_basis[...])
    for l in range(leaves):
        at = slice(l * panels, (l + 1) * panels)
        potential[:, at] = partial[:, at] + jnp.where(
            inside_of(count, l, panels), value[:, at], 0.0
        )


def call(kernel, name, outs, args, scalars, scratch=(), flops=1 << 20, moved=1 << 20):
    in_specs = [
        pl.BlockSpec(memory_space=pltpu.SMEM if k < scalars else pltpu.VMEM)
        for k in range(len(args))
    ]
    return pl.pallas_call(
        kernel,
        name=name,
        out_shape=[jax.ShapeDtypeStruct(s, f32) for s in outs],
        in_specs=in_specs,
        out_specs=[pl.BlockSpec(memory_space=pltpu.VMEM)] * len(outs),
        scratch_shapes=list(scratch),
        compiler_params=pltpu.CompilerParams(vmem_limit_bytes=48 * 2**20),
        cost_estimate=pl.CostEstimate(flops=flops, bytes_accessed=moved, transcendentals=0),
    )(*args)


def passed_along(value, axis, by):
    peers = lax.axis_size(axis)
    pairs = [(i, i + by) for i in range(peers) if 0 <= i + by < peers]
    return lax.ppermute(value, axis, pairs)


def shards(
    charges,
    centers,
    areas,
    panel_count,
    near_pairs,
    pair_count,
    basis,
    leaf_transfer,
    cluster_transfer,
    leaf_coupling,
    cluster_coupling,
    group_coupling,
):
    leaves, rank, panels = basis.shape
    sides, total = charges.shape
    width = 2 * leaves
    subs = lax.axis_size("sub")
    groups = lax.axis_size("grp")
    g = lax.axis_index("grp")
    s = lax.axis_index("sub")
    index = jnp.stack([g, s, (s < subs - 1).astype(jnp.int32)]).astype(jnp.int32)
    areas = areas.reshape(1, total)
    lt = leaf_transfer.reshape(leaves * rank, rank)
    ct = cluster_transfer.reshape(rank, rank)
    cc = cluster_coupling.reshape(rank, subs * rank)
    coupling = leaf_coupling.reshape(leaves * rank, width * rank)
    group = group_coupling.reshape(groups, rank, groups * rank)
    extra = leaves * rank

    z, x = call(
        upward,
        "upward",
        [(subs, sides // 2, LANES), (sides + 8, total + extra)],
        (index, panel_count, charges, areas, centers, basis, lt, ct, cc),
        2,
    )
    got = lax.all_to_all(z, "sub", 0, 0, tiled=True)
    x_next = passed_along(x, "sub", -1)
    near_own, lifted_basis, group_matrix = call(
        own_blocks,
        "own_blocks",
        [(sides, total), (rank, total), (groups * rank, rank)],
        (index, x, basis, lt, ct, group),
        1,
        flops=5 * 10**9,
    )
    near, out_next, far = call(
        window_blocks,
        "window_blocks",
        [(sides, total), (sides, total + extra), (sides, extra)],
        (index, near_pairs, pair_count, x, x_next, coupling),
        3,
        [
            pltpu.VMEM((width, 2 * sides, panels), bf16),
            pltpu.VMEM((width, 8, panels), f32),
            pltpu.VMEM((leaves, panels, 8), f32),
            pltpu.VMEM((width, sides, panels), f32),
            pltpu.VMEM(coupling.shape, f32),
        ],
        flops=10**10,
    )
    got_next = passed_along(out_next, "sub", 1)
    (group_sums,) = call(summed, "summed", [(groups, sides // 2, LANES)], (got,), 0)
    got_groups = lax.all_to_all(group_sums, "grp", 0, 0, tiled=True)
    cluster, partial = call(
        combined,
        "combined",
        [(sides, rank), (sides, total)],
        (index, panel_count, got, cc, near_own, near, far, got_next, areas, basis),
        2,
        flops=2 * 10**9,
    )
    (potential,) = call(
        finished,
        "finished",
        [(sides, total)],
        (panel_count, got_groups, cluster, group_matrix, lifted_basis, partial),
        1,
    )
    return potential


def solution(mesh):
    both = ("grp", "sub")
    return jax.shard_map(
        shards,
        mesh=mesh,
        in_specs=(
            P(None, both),
            P(None, both),
            P(both),
            P(both),
            P(None, both),
            P(both),
            P(both, None, None),
            P(both, None, None),
            P(both, None, None),
            P(both, None, None),
            P(both, None, None),
            P(),
        ),
        out_specs=P(None, both),
        check_vma=False,
    )
```
